32 devices in a mesh: ctx: 8 (over z, y), ch: 4 (over x, core).
Axes of the slice: x: 2, y: 2, z: 4, core: 2. Of those that a mesh axis runs over, the one named last changes fastest.
Arguments:
- q_li: bfloat16 [4096, 8192], P('ctx', 'ch'), may hold values from -6 to 6
- k_li: bfloat16 [4096, 8192], P('ctx', 'ch'), may hold values from -6 to 6
- v_li: bfloat16 [4096, 8192], P('ctx', 'ch'), may hold values from -6 to 6
- q_att: bfloat16 [4096, 8192], P('ctx', 'ch'), may hold values from -5 to 5
- k_att: bfloat16 [4096, 8192], P('ctx', 'ch'), may hold values from -5 to 5
- cotangent: bfloat16 [4096, 8192], P('ctx', 'ch'), may hold values from -6 to 6
- record_ids: int32 [4096], P('ctx'), may hold values from 0 to 7, never falling along the last dimension, each value on 1 to 1024 neighbouring positions
- decay_rate: float32 [16, 8192], P(None, 'ch'), may hold values from 2.4414062e-06 to 0.04
- residue: float32 [16, 8192], P(None, 'ch'), may hold values from -6 to 6
- norm_gain: float32 [8192], P('ch'), may hold values from 0.1 to 1.9
Outputs:
- attended: bfloat16 [4096, 8192], P('ctx', 'ch')
- d_q_att: bfloat16 [4096, 8192], P('ctx', 'ch')
- d_k_att: bfloat16 [4096, 8192], P('ctx', 'ch')
- d_q_li: bfloat16 [4096, 8192], P('ctx', 'ch')
- d_k_li: bfloat16 [4096, 8192], P('ctx', 'ch')
- d_v_li: bfloat16 [4096, 8192], P('ctx', 'ch')
The draws below stay inside these ranges and needn't reach their ends.
Inputs may be any that keep to these rules, and one draw needn't show every extreme that they name: `record_ids`: record numbers never fall along the sequence; every record holds 1 to 1024 positions, and some record holds exactly 1024.
All inputs are finite; a program needn't handle non-finite values.
Results may differ from the reference program's by a relative error of at most 0.017.
Values may be sent and summed in bfloat16 or wider, within the bound.
A program may use at most 320 MiB of HBM per device.

```python
import math
import jax
import jax.numpy as jnp
import numpy as np
from jax import lax

D = 8192
HEAD_DIM = 128
MODES = 16
SPAN = 2
TOK_DEV = 512
SEQ = 4096
RECORDS = 8
MOST = 1024
N_CTX = 8


def draw_q_att(key, part):
    key = jax.random.fold_in(key, 11)
    base = jnp.clip(jax.random.normal(key, (SEQ, D), jnp.float32), -5.0, 5.0)
    return base.astype(jnp.bfloat16)


def draw_k_att(key, part):
    key = jax.random.fold_in(key, 13)
    base = jnp.clip(jax.random.normal(key, (SEQ, D), jnp.float32), -5.0, 5.0)
    return base.astype(jnp.bfloat16)


def draw_residue(key, part):
    key = jax.random.fold_in(key, 5)
    shape_key, spread_key = jax.random.split(key)
    rising = jnp.power(3.0, jnp.arange(D, dtype=jnp.float32) / D - 0.5)
    spread = jnp.exp(jax.random.uniform(spread_key, (1, D), jnp.float32, -1.15, 1.15))
    base = jnp.clip(jax.random.normal(shape_key, (MODES, D), jnp.float32), -4.0, 4.0)
    return base * rising[None, :] * spread / 4.0


def level_of(own_key, shape, shards, smallest, top_value):
    level = 1.0
    for position, parts in shards:
        steps = jax.random.uniform(jax.random.fold_in(jax.random.fold_in(own_key, 6), position), (parts,), jnp.float32, smallest / len(shards), top_value / len(shards))
        level = level * jnp.repeat(jnp.exp(steps), shape[position] // parts).reshape((-1,) + (1,) * (len(shape) - 1 - position))
    return level


def split_up(amount, total, bound, slope):
    loads = [(1 << 20) // math.isqrt(standing ** slope) + 1 for standing in range(2, amount + 1)]
    surplus, counts = total - bound - (amount - 1), [1] * (amount - 1)
    while surplus > 0:
        free = [i for i in range(amount - 1) if counts[i] < bound]
        whole, left = sum([loads[i] for i in free]), surplus
        for i in free:
            extra = min(bound - counts[i], max(1, left * loads[i] // whole), surplus)
            counts[i] = counts[i] + extra
            surplus = surplus - extra
    return np.array([bound] + counts)


def ragged(key, amount, total, reach, lean):
    if amount == 2:
        one = jax.random.randint(key, (), max(1, total - reach), min(reach, total - 1) + 1)
        return jnp.stack([one, total - one])
    sizes = jnp.asarray(split_up(amount, total, reach, lean), jnp.int32)
    twos = (amount - 1) // 2
    giver, taker = sizes[1:1 + 2 * twos:2], sizes[2:2 + 2 * twos:2]
    room = jnp.minimum(giver - 1, reach - taker)
    moved = jax.random.randint(jax.random.fold_in(key, 1), (twos,), 0, 1 << 20) % (room + 1)
    sizes = sizes.at[1:1 + 2 * twos:2].set(giver - moved).at[2:2 + 2 * twos:2].set(taker + moved)
    return sizes[jax.random.permutation(jax.random.fold_in(key, 2), amount)]


def bell_draw(key, shape, scale, bound, cuts=(), held_as=jnp.bfloat16):
    values = scale * jax.random.normal(key, shape, jnp.float32)
    if cuts:
        values = values * level_of(key, shape, cuts, -0.22, 0.18)
    return jnp.clip(values, -bound, bound).astype(held_as)


def setup_inputs(seed: int = 0) -> dict:
    key_list = jax.random.split(jax.random.key(seed), 11)
    return {
        "q_li": bell_draw(key_list[0], (SEQ, D), 1.0, 6.0, ((0, 8), (1, 4))),
        "k_li": bell_draw(key_list[1], (SEQ, D), 1.0, 6.0, ((0, 8), (1, 4))),
        "v_li": bell_draw(key_list[2], (SEQ, D), 1.0, 6.0, ((0, 8), (1, 4))),
        "q_att": draw_q_att(jax.random.fold_in(key_list[10], 71), 0),
        "k_att": draw_k_att(jax.random.fold_in(key_list[10], 71), 0),
        "cotangent": bell_draw(key_list[5], (SEQ, D), 1.0, 6.0, ((0, 8), (1, 4))),
        "record_ids": jnp.searchsorted(jnp.cumsum(ragged(key_list[6], RECORDS, SEQ, MOST, 0)), jnp.arange(SEQ), side="right").astype(jnp.int32),
        "decay_rate": jnp.clip(jnp.exp(math.log(0.04) - 9.704061 * jax.random.uniform(key_list[7], (MODES, D), jnp.float32) ** level_of(key_list[7], (MODES, D), ((1, 4),), -0.2, 0.2)), 2.441406195430318e-06, 0.04),
        "residue": draw_residue(jax.random.fold_in(key_list[10], 71), 0),
        "norm_gain": jnp.clip(1.0 + 0.18 * jax.random.normal(key_list[9], (D,), jnp.float32), 0.1, 1.9),
    }


EPS = 1e-06
NEG = -1e+30

def filter_taps(rates, residues, length):
    inject = jnp.sqrt(-jnp.expm1(-2.0 * rates))
    steps_axis = jnp.arange(length, dtype=jnp.float32)[:, None]

    def add_mode(running, mode):
        rate_row, weight_row = mode
        return (running + weight_row[None, :] * jnp.exp(-rate_row[None, :] * steps_axis), None)
    filter_rows, unused = lax.scan(add_mode, jnp.zeros((length, rates.shape[1]), jnp.float32), (rates, residues * inject))
    return filter_rows

def causal_conv(signal, filter_rows):
    length = signal.shape[0]
    spectrum = jnp.fft.rfft(signal, 2 * length, axis=0) * jnp.fft.rfft(filter_rows, 2 * length, axis=0)
    return jnp.fft.irfft(spectrum, 2 * length, axis=0)[:length]

def channel_conv(signal, rates, residues, flipped):
    group_width = min(1024, signal.shape[1])

    def one_group(group_index):
        first_col = group_index * group_width
        section = lax.dynamic_slice_in_dim(signal, first_col, group_width, 1)
        filter_rows = filter_taps(lax.dynamic_slice_in_dim(rates, first_col, group_width, 1), lax.dynamic_slice_in_dim(residues, first_col, group_width, 1), signal.shape[0])
        if flipped:
            return causal_conv(section[::-1], filter_rows)[::-1]
        return causal_conv(section, filter_rows)
    pieces = lax.map(one_group, jnp.arange(signal.shape[1] // group_width, dtype=jnp.int32))
    return jnp.transpose(pieces, (1, 0, 2)).reshape(signal.shape)

def rounded(array):
    return lax.optimization_barrier(array.astype(jnp.bfloat16)).astype(jnp.float32)

def head_attention(queries, key_pad, value_pad, grads_out, query_ids, key_ids):
    pad_rows = SPAN * TOK_DEV
    window = (SPAN + 1) * TOK_DEV
    score_scale = HEAD_DIM ** (-0.5)

    def step_block(carry, block_index):
        key_acc, value_acc = carry
        start = block_index * TOK_DEV
        q_rows = lax.dynamic_slice_in_dim(queries, start, TOK_DEV, 0)
        g_rows = lax.dynamic_slice_in_dim(grads_out, start, TOK_DEV, 0)
        k_rows = lax.dynamic_slice_in_dim(key_pad, start, window, 0)
        v_rows = lax.dynamic_slice_in_dim(value_pad, start, window, 0)
        q_ids = lax.dynamic_slice_in_dim(query_ids, start, TOK_DEV, 0)
        k_ids = lax.dynamic_slice_in_dim(key_ids, start, window, 0)
        q_pos = start + jnp.arange(TOK_DEV, dtype=jnp.int32)
        k_pos = start - pad_rows + jnp.arange(window, dtype=jnp.int32)
        allowed = (q_ids[:, None] == k_ids[None, :]) & (k_pos[None, :] <= q_pos[:, None])
        scores = jnp.where(allowed, jnp.dot(q_rows, k_rows.T, preferred_element_type=jnp.float32) * score_scale, NEG)
        row_top = lax.optimization_barrier(jnp.max(scores, axis=1, keepdims=True))
        exponent = jnp.exp(scores - row_top)
        row_total = lax.optimization_barrier(jnp.sum(exponent, axis=1, keepdims=True))
        probs = exponent / row_total
        weights_low = probs.astype(jnp.bfloat16)
        output = jnp.dot(weights_low, v_rows, preferred_element_type=jnp.float32)
        row_delta = lax.optimization_barrier(jnp.sum(g_rows.astype(jnp.float32) * output, axis=1, keepdims=True))
        prob_grad = jnp.dot(g_rows, v_rows.T, preferred_element_type=jnp.float32)
        dscore = (probs * (prob_grad - row_delta)).astype(jnp.bfloat16)
        query_grad = jnp.dot(dscore, k_rows, preferred_element_type=jnp.float32) * score_scale
        key_part = rounded(jnp.dot(dscore.T, q_rows, preferred_element_type=jnp.float32) * score_scale)
        value_part = rounded(jnp.dot(weights_low.T, g_rows, preferred_element_type=jnp.float32))
        key_acc = lax.dynamic_update_slice_in_dim(key_acc, lax.dynamic_slice_in_dim(key_acc, start, window, 0) + key_part, start, 0)
        value_acc = lax.dynamic_update_slice_in_dim(value_acc, lax.dynamic_slice_in_dim(value_acc, start, window, 0) + value_part, start, 0)
        return ((key_acc, value_acc), (output.astype(jnp.bfloat16), query_grad.astype(jnp.bfloat16)))
    empty = jnp.zeros((pad_rows + SEQ, HEAD_DIM), jnp.float32)
    sums, emitted = lax.scan(step_block, (empty, empty), jnp.arange(N_CTX, dtype=jnp.int32))
    outputs = emitted[0].reshape(SEQ, HEAD_DIM)
    query_grads = emitted[1].reshape(SEQ, HEAD_DIM)
    return (outputs, query_grads, sums[0][pad_rows:], sums[1][pad_rows:])

def reference(q_li, k_li, v_li, q_att, k_att, cotangent, record_ids, decay_rate, residue, norm_gain):
    head_count = D // HEAD_DIM
    pad_rows = SPAN * TOK_DEV
    mixed_input = rounded(k_li.astype(jnp.float32) * v_li.astype(jnp.float32))
    mixed = channel_conv(mixed_input, decay_rate, residue, False)
    lifted = q_li.astype(jnp.float32) * mixed
    power = lax.optimization_barrier(jnp.sum(lifted * lifted, axis=1, keepdims=True)) / D
    inv_rms = lax.rsqrt(power + EPS)
    values = (lifted * inv_rms * norm_gain[None, :]).astype(jnp.bfloat16)

    def split_heads(array):
        return jnp.transpose(array.reshape(array.shape[0], head_count, HEAD_DIM), (1, 0, 2))

    def merge_heads(array):
        return jnp.transpose(array, (1, 0, 2)).reshape(array.shape[1], D)
    key_pad = jnp.concatenate([jnp.zeros((pad_rows, D), jnp.bfloat16), k_att], axis=0)
    value_pad = jnp.concatenate([jnp.zeros((pad_rows, D), jnp.bfloat16), values], axis=0)
    key_ids = jnp.concatenate([jnp.full((pad_rows,), -1, jnp.int32), record_ids], axis=0)

    def per_head(items):
        return head_attention(items[0], items[1], items[2], items[3], record_ids, key_ids)
    outputs, query_grads, key_sums, value_sums = lax.map(per_head, (split_heads(q_att), split_heads(key_pad), split_heads(value_pad), split_heads(cotangent)))
    attended = merge_heads(outputs)
    d_q_att = merge_heads(query_grads)
    d_k_att = merge_heads(key_sums).astype(jnp.bfloat16)
    value_sum = merge_heads(value_sums)
    weighted = value_sum * norm_gain[None, :]
    inner = lax.optimization_barrier(jnp.sum(lifted * weighted, axis=1, keepdims=True))
    lifted_grad = inv_rms * weighted - lifted * inv_rms ** 3 * inner / D
    d_q_li = (lifted_grad * mixed).astype(jnp.bfloat16)
    mixed_grad = rounded(lifted_grad * q_li.astype(jnp.float32))
    input_grad = channel_conv(mixed_grad, decay_rate, residue, True)
    d_k_li = (input_grad * v_li.astype(jnp.float32)).astype(jnp.bfloat16)
    d_v_li = (input_grad * k_li.astype(jnp.float32)).astype(jnp.bfloat16)
    return (attended, d_q_att, d_k_att, d_q_li, d_k_li, d_v_li)
```

```python
import functools
import math

import jax
import jax.numpy as jnp
from jax import lax
from jax.experimental import pallas as pl
from jax.experimental.pallas import tpu as pltpu
from jax.sharding import PartitionSpec as P

D = 8192
HEAD_DIM = 128
SPAN = 2
EPS = 1e-06
NEG = -1e30
LANES = 128
SUB = 8
QUERY_BLOCK = 256
MOST = 1024
GROUPS = 4
VMEM = 56 * 1024 * 1024

F32 = jnp.float32
BF16 = jnp.bfloat16


def shifted(value, axis, steps):
    count = lax.axis_size(axis)
    initial, last = (max(0, -steps), min(count, count - steps))
    return lax.ppermute(value, axis, [(source, source + steps) for source in range(initial, last)])


def params():
    return pltpu.CompilerParams(vmem_limit_bytes=VMEM)


def spread(store, tokens, column):
    for j in range(SUB):
        store[pl.ds(j, tokens, SUB), :] = column(slice(j * LANES, (j + 1) * LANES))


def end_scan(signal, decay_ref, end_ref, tokens, backward):
    modes = decay_ref.shape[1]
    decays = [decay_ref[0, n] for n in range(modes)]

    def step(s, states):
        t = tokens - 1 - s if backward else s
        x = signal[pl.ds(pl.multiple_of(t * SUB, SUB), SUB), :]
        return tuple(decays[n] * states[n] + x for n in range(modes))

    zero = jnp.zeros((SUB, LANES), F32)
    states = lax.fori_loop(0, tokens, step, (zero,) * modes, unroll=8)
    for n in range(modes):
        end_ref[0, n] = states[n]


def full_scan(signal, decay_ref, weight_ref, state_ref, tokens, backward):
    modes = decay_ref.shape[1]
    decays = [decay_ref[0, n] for n in range(modes)]
    weights = [weight_ref[0, n] for n in range(modes)]

    def step(s, states):
        t = tokens - 1 - s if backward else s
        rows = pl.ds(pl.multiple_of(t * SUB, SUB), SUB)
        x = signal[rows, :]
        states = tuple(decays[n] * states[n] + x for n in range(modes))
        terms = [weights[n] * states[n] for n in range(modes)]
        while len(terms) > 1:
            terms = [terms[i] + terms[i + 1] for i in range(0, len(terms), 2)]
        signal[rows, :] = terms[0]
        return states

    lax.fori_loop(0, tokens, step, tuple(state_ref[0, n] for n in range(modes)), unroll=4)


def forward_ends(k_ref, v_ref, decay_ref, end_ref, signal):
    tokens = k_ref.shape[0]
    spread(signal, tokens, lambda c: (k_ref[:, c].astype(F32) * v_ref[:, c].astype(F32)).astype(BF16).astype(F32))
    end_scan(signal, decay_ref, end_ref, tokens, False)


def forward_mix(k_ref, v_ref, q_ref, decay_ref, weight_ref, state_ref, mixed_ref, power_ref, signal):
    tokens = k_ref.shape[0]
    spread(signal, tokens, lambda c: (k_ref[:, c].astype(F32) * v_ref[:, c].astype(F32)).astype(BF16).astype(F32))
    full_scan(signal, decay_ref, weight_ref, state_ref, tokens, False)
    power = jnp.zeros((tokens, LANES), F32)
    for j in range(SUB):
        c = slice(j * LANES, (j + 1) * LANES)
        mixed = signal[pl.ds(j, tokens, SUB), :]
        mixed_ref[:, c] = mixed
        lifted = q_ref[:, c].astype(F32) * mixed
        power = power + lifted * lifted

    @pl.when(pl.program_id(0) == 0)
    def _():
        power_ref[...] = power

    @pl.when(pl.program_id(0) > 0)
    def _():
        power_ref[...] += power


def backward_ends(g_ref, decay_ref, end_ref, signal):
    tokens = g_ref.shape[0]
    spread(signal, tokens, lambda c: g_ref[:, c].astype(F32))
    end_scan(signal, decay_ref, end_ref, tokens, True)


def backward_mix(g_ref, k_ref, v_ref, decay_ref, weight_ref, state_ref, dk_ref, dv_ref, signal):
    tokens = k_ref.shape[0]
    spread(signal, tokens, lambda c: g_ref[:, c].astype(F32))
    full_scan(signal, decay_ref, weight_ref, state_ref, tokens, True)
    for j in range(SUB):
        c = slice(j * LANES, (j + 1) * LANES)
        grad = signal[pl.ds(j, tokens, SUB), :]
        dk_ref[:, c] = (grad * v_ref[:, c].astype(F32)).astype(BF16)
        dv_ref[:, c] = (grad * k_ref[:, c].astype(F32)).astype(BF16)


def conv_call(body, name, tokens, channels, modes, in_kinds, out_kinds, flops, arrays):
    width = SUB * LANES
    specs = {
        "wide": pl.BlockSpec((tokens, width), lambda i: (0, i)),
        "mode": pl.BlockSpec((1, modes, SUB, LANES), lambda i: (i, 0, 0, 0)),
        "row": pl.BlockSpec((tokens, LANES), lambda i: (0, 0)),
    }
    shapes = {
        "wide": (tokens, channels),
        "mode": (channels // width, modes, SUB, LANES),
        "row": (tokens, LANES),
    }
    return pl.pallas_call(
        body,
        grid=(channels // width,),
        in_specs=[specs[kind] for kind in in_kinds],
        out_specs=[specs[kind] for kind, _ in out_kinds],
        out_shape=[jax.ShapeDtypeStruct(shapes[kind], dtype) for kind, dtype in out_kinds],
        scratch_shapes=[pltpu.VMEM((tokens * SUB, LANES), F32)],
        compiler_params=params(),
        cost_estimate=pl.CostEstimate(
            flops=flops * tokens * channels * modes, bytes_accessed=12 * tokens * channels, transcendentals=0
        ),
        name=name,
    )(*arrays)


def carried_state(slab_rate, local_state, backward):
    slab_count = lax.axis_size("ctx")
    collected = lax.all_gather(local_state[None], "ctx", axis=0, tiled=True)
    position = lax.axis_index("ctx")
    others = jnp.arange(slab_count, dtype=jnp.int32)
    spacing = others - position - 1 if backward else position - 1 - others
    spacing = spacing.reshape((slab_count,) + (1,) * local_state.ndim)
    distances = jnp.maximum(spacing, 0).astype(F32)
    weights = jnp.where(spacing >= 0, jnp.exp(-slab_rate[None] * distances), 0.0)
    return jnp.sum(weights * collected, axis=0)


def dots(left, right, a, b):
    return lax.dot_general(left, right, (((a,), (b,)), ((), ())), preferred_element_type=F32)


def attention(count, tokens, span, chained, first_ref, start_ref, *refs):
    ins, refs = refs[: 4 + 2 * span], refs[4 + 2 * span :]
    if chained:
        refs = refs[2:]
    q_ref, g_ref = ins[:2]
    key_refs, value_refs = ins[2 : 3 + span], ins[3 + span :]
    out_ref, dq_ref = refs[:2]
    dk_refs, dv_refs = refs[2 : 3 + span], refs[3 + span : 4 + 2 * span]
    bias, keys, values, dkeys, dvalues = refs[4 + 2 * span :]
    total = (span + 1) * tokens
    base = span * tokens
    scale = HEAD_DIM ** (-0.5)
    rate = scale * math.log2(math.e)

    @pl.when(pl.program_id(0) == 0)
    def _():
        for low in range(0, total, tokens):
            place = low + lax.broadcasted_iota(jnp.int32, (tokens, tokens), 0)
            row = base + lax.broadcasted_iota(jnp.int32, (tokens, tokens), 1)
            allowed = (place >= start_ref[...]) & (place <= row)
            bias[low : low + tokens, :] = jnp.where(allowed, 0.0, NEG)

    for j in range(span + 1):
        keys[j * tokens : (j + 1) * tokens, :] = key_refs[j][...]
        values[j * tokens : (j + 1) * tokens, :] = value_refs[j][...]
    dkeys[...] = jnp.zeros_like(dkeys)
    dvalues[...] = jnp.zeros_like(dvalues)

    size = QUERY_BLOCK
    for block in range(tokens // size):
        rows = slice(block * size, (block + 1) * size)
        stop = base + (block + 1) * size
        most = min((MOST + size) // size, stop // size)

        def variant(pieces, rows=rows, stop=stop):
            span_keys = slice(stop - pieces * size, stop)
            q = q_ref[rows, :]
            g = g_ref[rows, :]
            k = keys[span_keys, :]
            v = values[span_keys, :]
            scores = dots(k, q, 1, 1) + bias[span_keys, rows]
            top = jnp.max(scores, axis=0, keepdims=True)
            exponent = jnp.exp2((scores - top) * rate)
            probs = exponent * (1.0 / jnp.sum(exponent, axis=0, keepdims=True))
            low = probs.astype(BF16)
            output = dots(v, low, 0, 0)
            delta = jnp.sum(g.astype(F32).T * output, axis=0, keepdims=True)
            dscore = (probs * (dots(v, g, 1, 1) - delta)).astype(BF16)
            out_ref[rows, :] = output.T.astype(BF16)
            dq_ref[rows, :] = (dots(k, dscore, 0, 0) * scale).T.astype(BF16)
            dkeys[span_keys, :] += dots(dscore, q, 1, 0)
            dvalues[span_keys, :] += dots(low, g, 1, 0)

        needed = stop // size - first_ref[block]
        for pieces in range(1, most + 1):
            hit = needed == pieces if pieces < most else needed >= pieces
            pl.when(hit)(functools.partial(variant, pieces))

    for j in range(span + 1):
        part = slice(j * tokens, (j + 1) * tokens)
        dk_refs[j][...] = (dkeys[part, :] * scale).astype(BF16)
        dv_refs[j][...] = dvalues[part, :].astype(BF16)


def attend(group, count, first, start, q_att, cotangent, key_list, value_list, previous):
    tokens, channels = q_att.shape
    span = len(key_list) - 1
    heads = count // HEAD_DIM
    offset = group * heads
    whole = pl.BlockSpec((tokens, HEAD_DIM), lambda h, f: (0, offset + h))
    piece = pl.BlockSpec((tokens, HEAD_DIM), lambda h, f: (0, h))
    ins = [pl.BlockSpec((1, tokens), lambda h, f: (0, 0)), whole, whole]
    for entry in key_list + value_list:
        ins.append(whole if entry.shape[1] == channels else piece)
    aliases = {}
    operands = [first, start, q_att, cotangent, *key_list, *value_list]
    if previous is not None:
        ins += [pl.BlockSpec(memory_space=pl.ANY)] * 2
        aliases = {len(operands): 0, len(operands) + 1: 1}
        operands += list(previous)
    wide = jax.ShapeDtypeStruct((tokens, channels), BF16)
    small = jax.ShapeDtypeStruct((tokens, count), BF16)
    total = (span + 1) * tokens
    results = pl.pallas_call(
        functools.partial(attention, count, tokens, span, previous is not None),
        grid_spec=pltpu.PrefetchScalarGridSpec(
            num_scalar_prefetch=1,
            grid=(heads,),
            in_specs=ins,
            out_specs=[whole, whole] + [piece] * (2 * span + 2),
            scratch_shapes=[
                pltpu.VMEM((total, tokens), F32),
                pltpu.VMEM((total, HEAD_DIM), BF16),
                pltpu.VMEM((total, HEAD_DIM), BF16),
                pltpu.VMEM((total, HEAD_DIM), F32),
                pltpu.VMEM((total, HEAD_DIM), F32),
            ],
        ),
        out_shape=[wide, wide] + [small] * (2 * span + 2),
        input_output_aliases=aliases,
        compiler_params=params(),
        cost_estimate=pl.CostEstimate(
            flops=12 * heads * tokens * total * HEAD_DIM,
            bytes_accessed=32 * tokens * count,
            transcendentals=heads * tokens * total,
        ),
        name=f"attention_{group}",
    )(*operands)
    return results[:2], results[2 : 3 + span], results[3 + span :]


def local(q_li, k_li, v_li, q_att, k_att, cotangent, record_ids, decay_rate, residue, norm_gain):
    tokens, channels = q_li.shape
    modes = decay_rate.shape[0]
    width = SUB * LANES
    groups = math.gcd(GROUPS, channels // HEAD_DIM)
    count = channels // groups

    def by_group(array):
        return jnp.transpose(array.reshape(modes, channels // width, SUB, LANES), (1, 0, 2, 3))

    rate = by_group(decay_rate)
    decay = jnp.exp(-rate)
    weight = by_group(residue) * jnp.sqrt(-jnp.expm1(-2.0 * rate))
    slab_rate = rate * tokens
    call = functools.partial(conv_call, tokens=tokens, channels=channels, modes=modes)

    marks = record_ids + 1
    all_marks = [shifted(marks, "ctx", d) for d in range(SPAN, 0, -1)] + [marks]
    all_marks = jnp.concatenate(all_marks)
    start = jnp.sum((all_marks[:, None] < marks[None, :]).astype(jnp.int32), axis=0)
    first = start[::QUERY_BLOCK] // QUERY_BLOCK
    start = start[None, :]

    cols = [slice(g * count, (g + 1) * count) for g in range(groups)]
    far_keys = [[shifted(k_att[:, c], "ctx", d) for d in range(SPAN, 0, -1)] for c in cols]

    (ends,) = call(
        forward_ends, "forward_ends", in_kinds=("wide", "wide", "mode"), out_kinds=(("mode", F32),),
        flops=2, arrays=(k_li, v_li, decay),
    )
    incoming = carried_state(slab_rate, ends, False)
    mixed, power = call(
        forward_mix, "forward_mix", in_kinds=("wide",) * 3 + ("mode",) * 3,
        out_kinds=(("wide", F32), ("row", F32)), flops=4,
        arrays=(k_li, v_li, q_li, decay, weight, incoming),
    )
    inv_rms = lax.rsqrt(lax.psum(jnp.sum(power, axis=1), "ch") / D + EPS)[:, None]
    gain = norm_gain[None, :]

    previous = None
    key_totals, value_totals = [], []
    for g, c in enumerate(cols):
        values = (q_li[:, c].astype(F32) * mixed[:, c] * inv_rms * gain[:, c]).astype(BF16)
        far_values = [shifted(values, "ctx", d) for d in range(SPAN, 0, -1)]
        previous, dks, dvs = attend(
            g, count, first, start, q_att, cotangent, far_keys[g] + [k_att], far_values + [values], previous
        )
        key_total = dks[SPAN].astype(F32)
        value_total = dvs[SPAN].astype(F32)
        for d in range(1, SPAN + 1):
            key_total = key_total + shifted(dks[SPAN - d], "ctx", -d).astype(F32)
            value_total = value_total + shifted(dvs[SPAN - d], "ctx", -d).astype(F32)
        key_totals.append(key_total.astype(BF16))
        value_totals.append(value_total)
    attended, d_q_att = previous
    d_k_att = jnp.concatenate(key_totals, axis=1)
    inner = jnp.zeros((tokens,), F32)
    for c, value_total in zip(cols, value_totals):
        lifted = q_li[:, c].astype(F32) * mixed[:, c]
        inner = inner + jnp.sum(lifted * value_total * gain[:, c], axis=1)
    inner = lax.psum(inner, "ch")[:, None]
    weighted = jnp.concatenate(value_totals, axis=1) * gain
    query = q_li.astype(F32)
    lifted_grad = inv_rms * weighted - query * mixed * (inv_rms**3) * inner / D
    d_q_li = (lifted_grad * mixed).astype(BF16)
    mixed_grad = (lifted_grad * query).astype(BF16)
    (starts,) = call(
        backward_ends, "backward_ends", in_kinds=("wide", "mode"), out_kinds=(("mode", F32),),
        flops=2, arrays=(mixed_grad, decay),
    )
    arriving = carried_state(slab_rate, starts, True)
    d_k_li, d_v_li = call(
        backward_mix, "backward_mix", in_kinds=("wide",) * 3 + ("mode",) * 3,
        out_kinds=(("wide", BF16), ("wide", BF16)), flops=4,
        arrays=(mixed_grad, k_li, v_li, decay, weight, arriving),
    )
    return (attended, d_q_att, d_k_att, d_q_li, d_k_li, d_v_li)


def solution(mesh):
    wide = P("ctx", "ch")
    return jax.shard_map(
        local,
        mesh=mesh,
        in_specs=(wide,) * 6 + (P("ctx"), P(None, "ch"), P(None, "ch"), P("ch")),
        out_specs=(wide,) * 6,
        check_vma=False,
    )
```

```python
import functools
import math

import jax
import jax.numpy as jnp
from jax import lax
from jax.experimental import pallas as pl
from jax.experimental.pallas import tpu as pltpu
from jax.sharding import PartitionSpec as P

D = 8192
HEAD_DIM = 128
SPAN = 2
EPS = 1e-06
NEG = -1e30
LANES = 128
SUB = 8
QUERY_BLOCK = 256
MOST = 1024
VMEM = 56 * 1024 * 1024

F32 = jnp.float32
BF16 = jnp.bfloat16


def shifted(value, axis, steps):
    count = lax.axis_size(axis)
    initial, last = (max(0, -steps), min(count, count - steps))
    return lax.ppermute(value, axis, [(source, source + steps) for source in range(initial, last)])


def params():
    return pltpu.CompilerParams(vmem_limit_bytes=VMEM)


def spread(store, tokens, column):
    for j in range(SUB):
        store[pl.ds(j, tokens, SUB), :] = column(slice(j * LANES, (j + 1) * LANES))


def end_scan(signal, decay_ref, end_ref, tokens, backward):
    modes = decay_ref.shape[1]
    decays = [decay_ref[0, n] for n in range(modes)]

    def step(s, states):
        t = tokens - 1 - s if backward else s
        x = signal[pl.ds(pl.multiple_of(t * SUB, SUB), SUB), :]
        return tuple(decays[n] * states[n] + x for n in range(modes))

    zero = jnp.zeros((SUB, LANES), F32)
    states = lax.fori_loop(0, tokens, step, (zero,) * modes, unroll=8)
    for n in range(modes):
        end_ref[0, n] = states[n]


def full_scan(signal, decay_ref, weight_ref, state_ref, tokens, backward):
    modes = decay_ref.shape[1]
    decays = [decay_ref[0, n] for n in range(modes)]
    weights = [weight_ref[0, n] for n in range(modes)]

    def step(s, states):
        t = tokens - 1 - s if backward else s
        rows = pl.ds(pl.multiple_of(t * SUB, SUB), SUB)
        x = signal[rows, :]
        states = tuple(decays[n] * states[n] + x for n in range(modes))
        terms = [weights[n] * states[n] for n in range(modes)]
        while len(terms) > 1:
            terms = [terms[i] + terms[i + 1] for i in range(0, len(terms), 2)]
        signal[rows, :] = terms[0]
        return states

    lax.fori_loop(0, tokens, step, tuple(state_ref[0, n] for n in range(modes)), unroll=4)


def forward_ends(k_ref, v_ref, decay_ref, end_ref, signal):
    tokens = k_ref.shape[0]
    spread(signal, tokens, lambda c: (k_ref[:, c].astype(F32) * v_ref[:, c].astype(F32)).astype(BF16).astype(F32))
    end_scan(signal, decay_ref, end_ref, tokens, False)


def forward_mix(k_ref, v_ref, q_ref, decay_ref, weight_ref, state_ref, mixed_ref, power_ref, signal):
    tokens = k_ref.shape[0]
    spread(signal, tokens, lambda c: (k_ref[:, c].astype(F32) * v_ref[:, c].astype(F32)).astype(BF16).astype(F32))
    full_scan(signal, decay_ref, weight_ref, state_ref, tokens, False)
    power = jnp.zeros((tokens, LANES), F32)
    for j in range(SUB):
        c = slice(j * LANES, (j + 1) * LANES)
        mixed = signal[pl.ds(j, tokens, SUB), :]
        mixed_ref[:, c] = mixed
        lifted = q_ref[:, c].astype(F32) * mixed
        power = power + lifted * lifted

    @pl.when(pl.program_id(0) == 0)
    def _():
        power_ref[...] = power

    @pl.when(pl.program_id(0) > 0)
    def _():
        power_ref[...] += power


def backward_ends(g_ref, decay_ref, end_ref, signal):
    tokens = g_ref.shape[0]
    spread(signal, tokens, lambda c: g_ref[:, c].astype(F32))
    end_scan(signal, decay_ref, end_ref, tokens, True)


def backward_mix(g_ref, k_ref, v_ref, decay_ref, weight_ref, state_ref, dk_ref, dv_ref, signal):
    tokens = k_ref.shape[0]
    spread(signal, tokens, lambda c: g_ref[:, c].astype(F32))
    full_scan(signal, decay_ref, weight_ref, state_ref, tokens, True)
    for j in range(SUB):
        c = slice(j * LANES, (j + 1) * LANES)
        grad = signal[pl.ds(j, tokens, SUB), :]
        dk_ref[:, c] = (grad * v_ref[:, c].astype(F32)).astype(BF16)
        dv_ref[:, c] = (grad * k_ref[:, c].astype(F32)).astype(BF16)


def conv_call(body, name, tokens, channels, modes, in_kinds, out_kinds, flops, arrays):
    width = SUB * LANES
    specs = {
        "wide": pl.BlockSpec((tokens, width), lambda i: (0, i)),
        "mode": pl.BlockSpec((1, modes, SUB, LANES), lambda i: (i, 0, 0, 0)),
        "row": pl.BlockSpec((tokens, LANES), lambda i: (0, 0)),
    }
    shapes = {
        "wide": (tokens, channels),
        "mode": (channels // width, modes, SUB, LANES),
        "row": (tokens, LANES),
    }
    return pl.pallas_call(
        body,
        grid=(channels // width,),
        in_specs=[specs[kind] for kind in in_kinds],
        out_specs=[specs[kind] for kind, _ in out_kinds],
        out_shape=[jax.ShapeDtypeStruct(shapes[kind], dtype) for kind, dtype in out_kinds],
        scratch_shapes=[pltpu.VMEM((tokens * SUB, LANES), F32)],
        compiler_params=params(),
        cost_estimate=pl.CostEstimate(
            flops=flops * tokens * channels * modes, bytes_accessed=12 * tokens * channels, transcendentals=0
        ),
        name=name,
    )(*arrays)


def carried_state(slab_rate, local_state, backward):
    slab_count = lax.axis_size("ctx")
    collected = lax.all_gather(local_state[None], "ctx", axis=0, tiled=True)
    position = lax.axis_index("ctx")
    others = jnp.arange(slab_count, dtype=jnp.int32)
    spacing = others - position - 1 if backward else position - 1 - others
    spacing = spacing.reshape((slab_count,) + (1,) * local_state.ndim)
    distances = jnp.maximum(spacing, 0).astype(F32)
    weights = jnp.where(spacing >= 0, jnp.exp(-slab_rate[None] * distances), 0.0)
    return jnp.sum(weights * collected, axis=0)


def dots(left, right, a, b):
    return lax.dot_general(left, right, (((a,), (b,)), ((), ())), preferred_element_type=F32)


def attention(tokens, heads, slabs, span, start_ref, q_ref, g_ref, *refs):
    key_refs, refs = refs[: span + 1], refs[span + 1 :]
    own_values, out_ref, dq_ref, dk_ref, dv_ref = refs[:5]
    bias, keys, values, dkeys, dvalues, far_values, sent, landed, own = refs[5:14]
    value_send, value_recv, grad_send, grad_recv = refs[14:]
    total = (span + 1) * tokens
    base = span * tokens
    scale = HEAD_DIM ** (-0.5)
    rate = scale * math.log2(math.e)
    step = pl.program_id(0)
    me = lax.axis_index("ctx")
    distances = range(span, 0, -1)

    def value_copy(d, h):
        return pltpu.make_async_remote_copy(
            src_ref=own_values.at[:, pl.ds(pl.multiple_of(h * HEAD_DIM, HEAD_DIM), HEAD_DIM)],
            dst_ref=far_values.at[d - 1, h],
            send_sem=value_send.at[d - 1, h],
            recv_sem=value_recv.at[d - 1, h],
            device_id={"ctx": lax.rem(me + d, slabs)},
            device_id_type=pl.DeviceIdType.MESH,
        )

    def grad_copy(kind, d, h):
        return pltpu.make_async_remote_copy(
            src_ref=sent.at[kind, d - 1, h],
            dst_ref=landed.at[kind, d - 1, h],
            send_sem=grad_send.at[kind, d - 1, h],
            recv_sem=grad_recv.at[kind, d - 1, h],
            device_id={"ctx": lax.rem(me - d + slabs, slabs)},
            device_id_type=pl.DeviceIdType.MESH,
        )

    @pl.when(step == 0)
    def _():
        barrier = pltpu.get_barrier_semaphore()
        partners = 0
        for d in distances:
            later, earlier = me + d < slabs, me >= d

            @pl.when(later)
            def _(d=d):
                pl.semaphore_signal(
                    barrier, inc=1, device_id={"ctx": lax.rem(me + d, slabs)}, device_id_type=pl.DeviceIdType.MESH
                )

            @pl.when(earlier)
            def _(d=d):
                pl.semaphore_signal(
                    barrier,
                    inc=1,
                    device_id={"ctx": lax.rem(me - d + slabs, slabs)},
                    device_id_type=pl.DeviceIdType.MESH,
                )

            partners = partners + later.astype(jnp.int32) + earlier.astype(jnp.int32)
        pl.semaphore_wait(barrier, partners)

        @pl.loop(0, heads)
        def _(h):
            for d in distances:
                pl.when(me + d < slabs)(lambda d=d: value_copy(d, h).start())

        for low in range(0, total, tokens):
            place = low + lax.broadcasted_iota(jnp.int32, (tokens, tokens), 0)
            row = base + lax.broadcasted_iota(jnp.int32, (tokens, tokens), 1)
            allowed = (place >= start_ref[...]) & (place <= row)
            bias[low : low + tokens, :] = jnp.where(allowed, 0.0, NEG)

    @pl.when(step < heads)
    def _():
        h = jnp.minimum(step, heads - 1)
        for d in distances:
            slab = slice((span - d) * tokens, (span - d + 1) * tokens)

            @pl.when(me >= d)
            def _(d=d, slab=slab):
                value_copy(d, h).wait_recv()
                values[slab, :] = far_values[d - 1, h]

            @pl.when(me < d)
            def _(d=d, slab=slab):
                values[slab, :] = jnp.zeros((tokens, HEAD_DIM), BF16)

        values[base:, :] = own_values[:, pl.ds(pl.multiple_of(h * HEAD_DIM, HEAD_DIM), HEAD_DIM)]
        for j in range(span + 1):
            keys[j * tokens : (j + 1) * tokens, :] = key_refs[j][...]
        dkeys[...] = jnp.zeros_like(dkeys)
        dvalues[...] = jnp.zeros_like(dvalues)
        size = QUERY_BLOCK
        for block in range(tokens // size):
            rows = slice(block * size, (block + 1) * size)
            stop = base + (block + 1) * size
            near = slice(max(0, stop - MOST - size), stop)
            q = q_ref[rows, :]
            g = g_ref[rows, :]
            k = keys[near, :]
            v = values[near, :]
            scores = dots(k, q, 1, 1) + bias[near, rows]
            top = jnp.max(scores, axis=0, keepdims=True)
            exponent = jnp.exp2((scores - top) * rate)
            probs = exponent * (1.0 / jnp.sum(exponent, axis=0, keepdims=True))
            low = probs.astype(BF16)
            output = dots(v, low, 0, 0)
            delta = jnp.sum(g.astype(F32).T * output, axis=0, keepdims=True)
            dscore = (probs * (dots(v, g, 1, 1) - delta)).astype(BF16)
            out_ref[rows, :] = output.T.astype(BF16)
            dq_ref[rows, :] = (dots(k, dscore, 0, 0) * scale).T.astype(BF16)
            dkeys[near, :] += dots(dscore, q, 1, 0)
            dvalues[near, :] += dots(low, g, 1, 0)

        for d in range(span, -1, -1):
            slab = slice((span - d) * tokens, (span - d + 1) * tokens)
            key_part = (dkeys[slab, :] * scale).astype(BF16)
            value_part = dvalues[slab, :].astype(BF16)
            if d == 0:
                own[0, h] = key_part
                own[1, h] = value_part
                continue

            @pl.when(me >= d)
            def _(d=d, key_part=key_part, value_part=value_part):
                sent[0, d - 1, h] = key_part
                sent[1, d - 1, h] = value_part
                grad_copy(0, d, h).start()
                grad_copy(1, d, h).start()

    @pl.when(step >= heads)
    def _():
        h = jnp.maximum(step - heads, 0)
        for d in distances:

            @pl.when(me + d < slabs)
            def _(d=d):
                value_copy(d, h).wait_send()
                grad_copy(0, d, h).wait_recv()
                grad_copy(1, d, h).wait_recv()

            @pl.when(me + d >= slabs)
            def _(d=d):
                for kind in range(2):
                    landed[kind, d - 1, h] = jnp.zeros((tokens, HEAD_DIM), BF16)

            @pl.when(me >= d)
            def _(d=d):
                grad_copy(0, d, h).wait_send()
                grad_copy(1, d, h).wait_send()

        sums = [own[kind, h].astype(F32) for kind in range(2)]
        for d in range(1, span + 1):
            sums = [sums[kind] + landed[kind, d - 1, h].astype(F32) for kind in range(2)]
        dk_ref[...] = sums[0].astype(BF16)
        dv_ref[...] = sums[1]


def attend(start, q_att, cotangent, key_list, values, slabs):
    tokens, channels = q_att.shape
    span = len(key_list) - 1
    heads = channels // HEAD_DIM
    first = pl.BlockSpec((tokens, HEAD_DIM), lambda h: (0, jnp.minimum(h, heads - 1)))
    second = pl.BlockSpec((tokens, HEAD_DIM), lambda h: (0, jnp.maximum(h - heads, 0)))
    total = (span + 1) * tokens
    low = jax.ShapeDtypeStruct((tokens, channels), BF16)
    return pl.pallas_call(
        functools.partial(attention, tokens, heads, slabs, span),
        grid=(2 * heads,),
        in_specs=[pl.BlockSpec((1, tokens), lambda h: (0, 0))]
        + [first] * (3 + span)
        + [pl.BlockSpec(memory_space=pltpu.VMEM)],
        out_specs=[first, first, second, second],
        out_shape=[low, low, low, jax.ShapeDtypeStruct((tokens, channels), F32)],
        scratch_shapes=[
            pltpu.VMEM((total, tokens), F32),
            pltpu.VMEM((total, HEAD_DIM), BF16),
            pltpu.VMEM((total, HEAD_DIM), BF16),
            pltpu.VMEM((total, HEAD_DIM), F32),
            pltpu.VMEM((total, HEAD_DIM), F32),
            pltpu.VMEM((span, heads, tokens, HEAD_DIM), BF16),
            pltpu.VMEM((2, span, heads, tokens, HEAD_DIM), BF16),
            pltpu.VMEM((2, span, heads, tokens, HEAD_DIM), BF16),
            pltpu.VMEM((2, heads, tokens, HEAD_DIM), BF16),
            pltpu.SemaphoreType.DMA((span, heads)),
            pltpu.SemaphoreType.DMA((span, heads)),
            pltpu.SemaphoreType.DMA((2, span, heads)),
            pltpu.SemaphoreType.DMA((2, span, heads)),
        ],
        compiler_params=pltpu.CompilerParams(vmem_limit_bytes=VMEM, collective_id=0, has_side_effects=True),
        cost_estimate=pl.CostEstimate(
            flops=12 * heads * tokens * total * HEAD_DIM,
            bytes_accessed=32 * tokens * channels,
            transcendentals=heads * tokens * total,
        ),
        name="attention",
    )(start, q_att, cotangent, *key_list, values)


def local(q_li, k_li, v_li, q_att, k_att, cotangent, record_ids, decay_rate, residue, norm_gain):
    tokens, channels = q_li.shape
    modes = decay_rate.shape[0]
    width = SUB * LANES

    def by_group(array):
        return jnp.transpose(array.reshape(modes, channels // width, SUB, LANES), (1, 0, 2, 3))

    rate = by_group(decay_rate)
    decay = jnp.exp(-rate)
    weight = by_group(residue) * jnp.sqrt(-jnp.expm1(-2.0 * rate))
    slab_rate = rate * tokens
    call = functools.partial(conv_call, tokens=tokens, channels=channels, modes=modes)

    marks = record_ids + 1
    all_marks = [shifted(marks, "ctx", d) for d in range(SPAN, 0, -1)] + [marks]
    all_marks = jnp.concatenate(all_marks)
    start = jnp.sum((all_marks[:, None] < marks[None, :]).astype(jnp.int32), axis=0)
    start = start[None, :]
    key_list = [shifted(k_att, "ctx", d) for d in range(SPAN, 0, -1)] + [k_att]

    (ends,) = call(
        forward_ends, "forward_ends", in_kinds=("wide", "wide", "mode"), out_kinds=(("mode", F32),),
        flops=2, arrays=(k_li, v_li, decay),
    )
    incoming = carried_state(slab_rate, ends, False)
    mixed, power = call(
        forward_mix, "forward_mix", in_kinds=("wide",) * 3 + ("mode",) * 3,
        out_kinds=(("wide", F32), ("row", F32)), flops=4,
        arrays=(k_li, v_li, q_li, decay, weight, incoming),
    )
    inv_rms = lax.rsqrt(lax.psum(jnp.sum(power, axis=1), "ch") / D + EPS)[:, None]
    gain = norm_gain[None, :]

    values = (q_li.astype(F32) * mixed * inv_rms * gain).astype(BF16)
    attended, d_q_att, d_k_att, value_total = attend(
        start, q_att, cotangent, key_list, values, lax.axis_size("ctx")
    )
    weighted = value_total * gain
    inner = lax.psum(jnp.sum(q_li.astype(F32) * mixed * weighted, axis=1), "ch")[:, None]
    query = q_li.astype(F32)
    lifted_grad = inv_rms * weighted - query * mixed * (inv_rms**3) * inner / D
    d_q_li = (lifted_grad * mixed).astype(BF16)
    mixed_grad = (lifted_grad * query).astype(BF16)
    (starts,) = call(
        backward_ends, "backward_ends", in_kinds=("wide", "mode"), out_kinds=(("mode", F32),),
        flops=2, arrays=(mixed_grad, decay),
    )
    arriving = carried_state(slab_rate, starts, True)
    d_k_li, d_v_li = call(
        backward_mix, "backward_mix", in_kinds=("wide",) * 3 + ("mode",) * 3,
        out_kinds=(("wide", BF16), ("wide", BF16)), flops=4,
        arrays=(mixed_grad, k_li, v_li, decay, weight, arriving),
    )
    return (attended, d_q_att, d_k_att, d_q_li, d_k_li, d_v_li)


def solution(mesh):
    wide = P("ctx", "ch")
    return jax.shard_map(
        local,
        mesh=mesh,
        in_specs=(wide,) * 6 + (P("ctx"), P(None, "ch"), P(None, "ch"), P("ch")),
        out_specs=(wide,) * 6,
        check_vma=False,
    )
```

```python
import functools
import math

import jax
import jax.numpy as jnp
from jax import lax
from jax.experimental import pallas as pl
from jax.experimental.pallas import tpu as pltpu
from jax.sharding import PartitionSpec as P

D = 8192
HEAD_DIM = 128
SPAN = 2
EPS = 1e-06
NEG = -1e30
LANES = 128
SUB = 8
QUERY_BLOCK = 256
MOST = 1024
VMEM = 56 * 1024 * 1024

F32 = jnp.float32
BF16 = jnp.bfloat16


def shifted(value, axis, steps):
    count = lax.axis_size(axis)
    initial, last = (max(0, -steps), min(count, count - steps))
    return lax.ppermute(value, axis, [(source, source + steps) for source in range(initial, last)])


def params():
    return pltpu.CompilerParams(vmem_limit_bytes=VMEM)


def spread(store, tokens, column):
    for j in range(SUB):
        store[pl.ds(j, tokens, SUB), :] = column(slice(j * LANES, (j + 1) * LANES))


def end_scan(signal, decay_ref, end_ref, tokens, backward):
    modes = decay_ref.shape[1]
    decays = [decay_ref[0, n] for n in range(modes)]

    def step(s, states):
        t = tokens - 1 - s if backward else s
        x = signal[pl.ds(pl.multiple_of(t * SUB, SUB), SUB), :]
        return tuple(decays[n] * states[n] + x for n in range(modes))

    zero = jnp.zeros((SUB, LANES), F32)
    states = lax.fori_loop(0, tokens, step, (zero,) * modes, unroll=8)
    for n in range(modes):
        end_ref[0, n] = states[n]


def full_scan(signal, decay_ref, weight_ref, state_ref, tokens, backward):
    modes = decay_ref.shape[1]
    decays = [decay_ref[0, n] for n in range(modes)]
    weights = [weight_ref[0, n] for n in range(modes)]

    def step(s, states):
        t = tokens - 1 - s if backward else s
        rows = pl.ds(pl.multiple_of(t * SUB, SUB), SUB)
        x = signal[rows, :]
        states = tuple(decays[n] * states[n] + x for n in range(modes))
        terms = [weights[n] * states[n] for n in range(modes)]
        while len(terms) > 1:
            terms = [terms[i] + terms[i + 1] for i in range(0, len(terms), 2)]
        signal[rows, :] = terms[0]
        return states

    lax.fori_loop(0, tokens, step, tuple(state_ref[0, n] for n in range(modes)), unroll=4)


def forward_ends(k_ref, v_ref, decay_ref, end_ref, signal):
    tokens = k_ref.shape[0]
    spread(signal, tokens, lambda c: (k_ref[:, c].astype(F32) * v_ref[:, c].astype(F32)).astype(BF16).astype(F32))
    end_scan(signal, decay_ref, end_ref, tokens, False)


def forward_mix(k_ref, v_ref, q_ref, decay_ref, weight_ref, state_ref, mixed_ref, power_ref, signal):
    tokens = k_ref.shape[0]
    spread(signal, tokens, lambda c: (k_ref[:, c].astype(F32) * v_ref[:, c].astype(F32)).astype(BF16).astype(F32))
    full_scan(signal, decay_ref, weight_ref, state_ref, tokens, False)
    power = jnp.zeros((tokens, LANES), F32)
    for j in range(SUB):
        c = slice(j * LANES, (j + 1) * LANES)
        mixed = signal[pl.ds(j, tokens, SUB), :]
        mixed_ref[:, c] = mixed
        lifted = q_ref[:, c].astype(F32) * mixed
        power = power + lifted * lifted

    @pl.when(pl.program_id(0) == 0)
    def _():
        power_ref[...] = power

    @pl.when(pl.program_id(0) > 0)
    def _():
        power_ref[...] += power


def backward_ends(g_ref, decay_ref, end_ref, signal):
    tokens = g_ref.shape[0]
    spread(signal, tokens, lambda c: g_ref[:, c].astype(F32))
    end_scan(signal, decay_ref, end_ref, tokens, True)


def backward_mix(g_ref, k_ref, v_ref, decay_ref, weight_ref, state_ref, dk_ref, dv_ref, signal):
    tokens = k_ref.shape[0]
    spread(signal, tokens, lambda c: g_ref[:, c].astype(F32))
    full_scan(signal, decay_ref, weight_ref, state_ref, tokens, True)
    for j in range(SUB):
        c = slice(j * LANES, (j + 1) * LANES)
        grad = signal[pl.ds(j, tokens, SUB), :]
        dk_ref[:, c] = (grad * v_ref[:, c].astype(F32)).astype(BF16)
        dv_ref[:, c] = (grad * k_ref[:, c].astype(F32)).astype(BF16)


def conv_call(body, name, tokens, channels, modes, in_kinds, out_kinds, flops, arrays):
    width = SUB * LANES
    specs = {
        "wide": pl.BlockSpec((tokens, width), lambda i: (0, i)),
        "mode": pl.BlockSpec((1, modes, SUB, LANES), lambda i: (i, 0, 0, 0)),
        "row": pl.BlockSpec((tokens, LANES), lambda i: (0, 0)),
    }
    shapes = {
        "wide": (tokens, channels),
        "mode": (channels // width, modes, SUB, LANES),
        "row": (tokens, LANES),
    }
    return pl.pallas_call(
        body,
        grid=(channels // width,),
        in_specs=[specs[kind] for kind in in_kinds],
        out_specs=[specs[kind] for kind, _ in out_kinds],
        out_shape=[jax.ShapeDtypeStruct(shapes[kind], dtype) for kind, dtype in out_kinds],
        scratch_shapes=[pltpu.VMEM((tokens * SUB, LANES), F32)],
        compiler_params=params(),
        cost_estimate=pl.CostEstimate(
            flops=flops * tokens * channels * modes, bytes_accessed=12 * tokens * channels, transcendentals=0
        ),
        name=name,
    )(*arrays)


def carried_state(slab_rate, local_state, backward):
    slab_count = lax.axis_size("ctx")
    collected = lax.all_gather(local_state[None], "ctx", axis=0, tiled=True)
    position = lax.axis_index("ctx")
    others = jnp.arange(slab_count, dtype=jnp.int32)
    spacing = others - position - 1 if backward else position - 1 - others
    spacing = spacing.reshape((slab_count,) + (1,) * local_state.ndim)
    distances = jnp.maximum(spacing, 0).astype(F32)
    weights = jnp.where(spacing >= 0, jnp.exp(-slab_rate[None] * distances), 0.0)
    return jnp.sum(weights * collected, axis=0)


def dots(left, right, a, b):
    return lax.dot_general(left, right, (((a,), (b,)), ((), ())), preferred_element_type=F32)


def attention(tokens, heads, slabs, span, start_ref, q_ref, g_ref, *refs):
    own_keys, own_values, out_ref, dq_ref, dk_ref, dv_ref = refs[:6]
    bias, keys, values, dkeys, dvalues, far, sent, landed, own = refs[6:15]
    far_send, far_recv, grad_send, grad_recv = refs[15:]
    total = (span + 1) * tokens
    base = span * tokens
    scale = HEAD_DIM ** (-0.5)
    rate = scale * math.log2(math.e)
    step = pl.program_id(0)
    me = lax.axis_index("ctx")
    distances = range(span, 0, -1)

    def far_copy(kind, d, h):
        return pltpu.make_async_remote_copy(
            src_ref=(own_keys, own_values)[kind].at[:, pl.ds(pl.multiple_of(h * HEAD_DIM, HEAD_DIM), HEAD_DIM)],
            dst_ref=far.at[kind, d - 1, h],
            send_sem=far_send.at[kind, d - 1, h],
            recv_sem=far_recv.at[kind, d - 1, h],
            device_id={"ctx": lax.rem(me + d, slabs)},
            device_id_type=pl.DeviceIdType.MESH,
        )

    def grad_copy(kind, d, h):
        return pltpu.make_async_remote_copy(
            src_ref=sent.at[kind, d - 1, h],
            dst_ref=landed.at[kind, d - 1, h],
            send_sem=grad_send.at[kind, d - 1, h],
            recv_sem=grad_recv.at[kind, d - 1, h],
            device_id={"ctx": lax.rem(me - d + slabs, slabs)},
            device_id_type=pl.DeviceIdType.MESH,
        )

    @pl.when(step == 0)
    def _():
        barrier = pltpu.get_barrier_semaphore()
        partners = 0
        for d in distances:
            later, earlier = me + d < slabs, me >= d

            @pl.when(later)
            def _(d=d):
                pl.semaphore_signal(
                    barrier, inc=1, device_id={"ctx": lax.rem(me + d, slabs)}, device_id_type=pl.DeviceIdType.MESH
                )

            @pl.when(earlier)
            def _(d=d):
                pl.semaphore_signal(
                    barrier,
                    inc=1,
                    device_id={"ctx": lax.rem(me - d + slabs, slabs)},
                    device_id_type=pl.DeviceIdType.MESH,
                )

            partners = partners + later.astype(jnp.int32) + earlier.astype(jnp.int32)
        pl.semaphore_wait(barrier, partners)

        @pl.loop(0, heads)
        def _(h):
            for d in distances:

                @pl.when(me + d < slabs)
                def _(d=d):
                    far_copy(0, d, h).start()
                    far_copy(1, d, h).start()

        for low in range(0, total, tokens):
            place = low + lax.broadcasted_iota(jnp.int32, (tokens, tokens), 0)
            row = base + lax.broadcasted_iota(jnp.int32, (tokens, tokens), 1)
            allowed = (place >= start_ref[...]) & (place <= row)
            bias[low : low + tokens, :] = jnp.where(allowed, 0.0, NEG)

    @pl.when(step < heads)
    def _():
        h = jnp.minimum(step, heads - 1)
        for d in distances:
            slab = slice((span - d) * tokens, (span - d + 1) * tokens)

            @pl.when(me >= d)
            def _(d=d, slab=slab):
                far_copy(0, d, h).wait_recv()
                far_copy(1, d, h).wait_recv()
                keys[slab, :] = far[0, d - 1, h]
                values[slab, :] = far[1, d - 1, h]

            @pl.when(me < d)
            def _(d=d, slab=slab):
                keys[slab, :] = jnp.zeros((tokens, HEAD_DIM), BF16)
                values[slab, :] = jnp.zeros((tokens, HEAD_DIM), BF16)

        head = pl.ds(pl.multiple_of(h * HEAD_DIM, HEAD_DIM), HEAD_DIM)
        keys[base:, :] = own_keys[:, head]
        values[base:, :] = own_values[:, head]
        dkeys[...] = jnp.zeros_like(dkeys)
        dvalues[...] = jnp.zeros_like(dvalues)
        size = QUERY_BLOCK
        for block in range(tokens // size):
            rows = slice(block * size, (block + 1) * size)
            stop = base + (block + 1) * size
            near = slice(max(0, stop - MOST - size), stop)
            q = q_ref[rows, :]
            g = g_ref[rows, :]
            k = keys[near, :]
            v = values[near, :]
            scores = dots(k, q, 1, 1) + bias[near, rows]
            top = jnp.max(scores, axis=0, keepdims=True)
            exponent = jnp.exp2((scores - top) * rate)
            probs = exponent * (1.0 / jnp.sum(exponent, axis=0, keepdims=True))
            low = probs.astype(BF16)
            output = dots(v, low, 0, 0)
            delta = jnp.sum(g.astype(F32).T * output, axis=0, keepdims=True)
            dscore = (probs * (dots(v, g, 1, 1) - delta)).astype(BF16)
            out_ref[rows, :] = output.T.astype(BF16)
            dq_ref[rows, :] = (dots(k, dscore, 0, 0) * scale).T.astype(BF16)
            dkeys[near, :] += dots(dscore, q, 1, 0)
            dvalues[near, :] += dots(low, g, 1, 0)

        for d in range(span, -1, -1):
            slab = slice((span - d) * tokens, (span - d + 1) * tokens)
            key_part = (dkeys[slab, :] * scale).astype(BF16)
            value_part = dvalues[slab, :].astype(BF16)
            if d == 0:
                own[0, h] = key_part
                own[1, h] = value_part
                continue

            @pl.when(me >= d)
            def _(d=d, key_part=key_part, value_part=value_part):
                sent[0, d - 1, h] = key_part
                sent[1, d - 1, h] = value_part
                grad_copy(0, d, h).start()
                grad_copy(1, d, h).start()

    @pl.when(step >= heads)
    def _():
        h = jnp.maximum(step - heads, 0)
        for d in distances:

            @pl.when(me + d < slabs)
            def _(d=d):
                far_copy(0, d, h).wait_send()
                far_copy(1, d, h).wait_send()
                grad_copy(0, d, h).wait_recv()
                grad_copy(1, d, h).wait_recv()

            @pl.when(me + d >= slabs)
            def _(d=d):
                for kind in range(2):
                    landed[kind, d - 1, h] = jnp.zeros((tokens, HEAD_DIM), BF16)

            @pl.when(me >= d)
            def _(d=d):
                grad_copy(0, d, h).wait_send()
                grad_copy(1, d, h).wait_send()

        sums = [own[kind, h].astype(F32) for kind in range(2)]
        for d in range(1, span + 1):
            sums = [sums[kind] + landed[kind, d - 1, h].astype(F32) for kind in range(2)]
        dk_ref[...] = sums[0].astype(BF16)
        dv_ref[...] = sums[1]


def attend(start, q_att, cotangent, k_att, values, slabs):
    tokens, channels = q_att.shape
    span = SPAN
    heads = channels // HEAD_DIM
    first = pl.BlockSpec((tokens, HEAD_DIM), lambda h: (0, jnp.minimum(h, heads - 1)))
    second = pl.BlockSpec((tokens, HEAD_DIM), lambda h: (0, jnp.maximum(h - heads, 0)))
    total = (span + 1) * tokens
    low = jax.ShapeDtypeStruct((tokens, channels), BF16)
    return pl.pallas_call(
        functools.partial(attention, tokens, heads, slabs, span),
        grid=(2 * heads,),
        in_specs=[pl.BlockSpec((1, tokens), lambda h: (0, 0))]
        + [first] * 2
        + [pl.BlockSpec(memory_space=pltpu.VMEM)] * 2,
        out_specs=[first, first, second, second],
        out_shape=[low, low, low, jax.ShapeDtypeStruct((tokens, channels), F32)],
        scratch_shapes=[
            pltpu.VMEM((total, tokens), F32),
            pltpu.VMEM((total, HEAD_DIM), BF16),
            pltpu.VMEM((total, HEAD_DIM), BF16),
            pltpu.VMEM((total, HEAD_DIM), F32),
            pltpu.VMEM((total, HEAD_DIM), F32),
            pltpu.VMEM((2, span, heads, tokens, HEAD_DIM), BF16),
            pltpu.VMEM((2, span, heads, tokens, HEAD_DIM), BF16),
            pltpu.VMEM((2, span, heads, tokens, HEAD_DIM), BF16),
            pltpu.VMEM((2, heads, tokens, HEAD_DIM), BF16),
            pltpu.SemaphoreType.DMA((2, span, heads)),
            pltpu.SemaphoreType.DMA((2, span, heads)),
            pltpu.SemaphoreType.DMA((2, span, heads)),
            pltpu.SemaphoreType.DMA((2, span, heads)),
        ],
        compiler_params=pltpu.CompilerParams(vmem_limit_bytes=VMEM, collective_id=0, has_side_effects=True),
        cost_estimate=pl.CostEstimate(
            flops=12 * heads * tokens * total * HEAD_DIM,
            bytes_accessed=32 * tokens * channels,
            transcendentals=heads * tokens * total,
        ),
        name="attention",
    )(start, q_att, cotangent, k_att, values)


def local(q_li, k_li, v_li, q_att, k_att, cotangent, record_ids, decay_rate, residue, norm_gain):
    tokens, channels = q_li.shape
    modes = decay_rate.shape[0]
    width = SUB * LANES

    def by_group(array):
        return jnp.transpose(array.reshape(modes, channels // width, SUB, LANES), (1, 0, 2, 3))

    rate = by_group(decay_rate)
    decay = jnp.exp(-rate)
    weight = by_group(residue) * jnp.sqrt(-jnp.expm1(-2.0 * rate))
    slab_rate = rate * tokens
    call = functools.partial(conv_call, tokens=tokens, channels=channels, modes=modes)

    marks = record_ids + 1
    all_marks = [shifted(marks, "ctx", d) for d in range(SPAN, 0, -1)] + [marks]
    all_marks = jnp.concatenate(all_marks)
    start = jnp.sum((all_marks[:, None] < marks[None, :]).astype(jnp.int32), axis=0)
    start = start[None, :]

    (ends,) = call(
        forward_ends, "forward_ends", in_kinds=("wide", "wide", "mode"), out_kinds=(("mode", F32),),
        flops=2, arrays=(k_li, v_li, decay),
    )
    incoming = carried_state(slab_rate, ends, False)
    mixed, power = call(
        forward_mix, "forward_mix", in_kinds=("wide",) * 3 + ("mode",) * 3,
        out_kinds=(("wide", F32), ("row", F32)), flops=4,
        arrays=(k_li, v_li, q_li, decay, weight, incoming),
    )
    inv_rms = lax.rsqrt(lax.psum(jnp.sum(power, axis=1), "ch") / D + EPS)[:, None]
    gain = norm_gain[None, :]

    values = (q_li.astype(F32) * mixed * inv_rms * gain).astype(BF16)
    attended, d_q_att, d_k_att, value_total = attend(
        start, q_att, cotangent, k_att, values, lax.axis_size("ctx")
    )
    weighted = value_total * gain
    inner = lax.psum(jnp.sum(q_li.astype(F32) * mixed * weighted, axis=1), "ch")[:, None]
    query = q_li.astype(F32)
    lifted_grad = inv_rms * weighted - query * mixed * (inv_rms**3) * inner / D
    d_q_li = (lifted_grad * mixed).astype(BF16)
    mixed_grad = (lifted_grad * query).astype(BF16)
    (starts,) = call(
        backward_ends, "backward_ends", in_kinds=("wide", "mode"), out_kinds=(("mode", F32),),
        flops=2, arrays=(mixed_grad, decay),
    )
    arriving = carried_state(slab_rate, starts, True)
    d_k_li, d_v_li = call(
        backward_mix, "backward_mix", in_kinds=("wide",) * 3 + ("mode",) * 3,
        out_kinds=(("wide", BF16), ("wide", BF16)), flops=4,
        arrays=(mixed_grad, k_li, v_li, decay, weight, arriving),
    )
    return (attended, d_q_att, d_k_att, d_q_li, d_k_li, d_v_li)


def solution(mesh):
    wide = P("ctx", "ch")
    return jax.shard_map(
        local,
        mesh=mesh,
        in_specs=(wide,) * 6 + (P("ctx"), P(None, "ch"), P(None, "ch"), P("ch")),
        out_specs=(wide,) * 6,
        check_vma=False,
    )
```
